32 devices in a mesh: dp: 2 (over y), seq: 16 (over z, x, core).
Axes of the slice: x: 2, y: 2, z: 4, core: 2. Of those that a mesh axis runs over, the one named last changes fastest.
Arguments:
- queries: bfloat16 [2, 1024, 8192], P('dp', 'seq'), may hold values from -8 to 8
- keys: bfloat16 [2, 1024, 1024], P('dp', 'seq'), may hold values from -8 to 8
- values: bfloat16 [2, 1024, 1024], P('dp', 'seq'), may hold values from -6 to 6
- doc_lengths: int32 [2, 129], replicated, may hold values from 0 to 512, as said below
Outputs:
- attended: bfloat16 [2, 1024, 8192], P('dp', 'seq')
The draws below stay inside these ranges and needn't reach their ends.
Inputs may be any that keep to these rules, and one draw needn't show every extreme that they name: `doc_lengths`: each row sums to 1024; zeros stand only after the last document; the first document of every row has 32 tokens and the second exactly 512.
All inputs are finite; a program needn't handle non-finite values.
Results may differ from the reference program's by a relative error of at most 0.0045.
Values may be sent and summed in bfloat16 or wider, within the bound.
No kernel may reach another device: no remote copies, remote signals or barrier semaphores. Data moves between devices by JAX's collectives and lax.ppermute only.
A program may use at most 64 MiB of HBM per device.

```python
import math
import jax
import jax.numpy as jnp
from jax import lax

QH = 64
KVH = 8
HD = 128
TOK_DEV = 64
GROUP = 8
SEQS = 2
LEN = 1024
MAXDOC = 512
DOCS = 129


def draw_queries(key, part):
    drawn = jnp.clip(jax.random.normal(jax.random.fold_in(key, 1), (SEQS, LEN, QH * HD), jnp.float32), -4.5, 4.5)
    return drawn.astype(jnp.bfloat16)


def draw_keys(key, part):
    drawn = jnp.clip(jax.random.normal(jax.random.fold_in(key, 2), (SEQS, LEN, KVH * HD), jnp.float32), -4.5, 4.5)
    return drawn.astype(jnp.bfloat16)


def draw_doc_lengths(key, part):
    scale_key, raw_key = jax.random.split(jax.random.fold_in(key, 5))
    lowest = max(1, MAXDOC // 64)
    level = jax.random.randint(scale_key, (SEQS, 1), 0, 6)
    typical = jnp.right_shift(jnp.full((SEQS, 1), MAXDOC, jnp.int32), level.astype(jnp.int32))
    low_end = jnp.maximum(typical // 2, lowest)
    high_end = jnp.minimum(2 * typical, MAXDOC)
    spread = jax.random.randint(raw_key, (SEQS, DOCS), 0, 1 << 20)
    raw = low_end + spread % (high_end - low_end + 1)
    raw = raw.at[:, 0].set(max(1, TOK_DEV // 2))
    raw = raw.at[:, 1].set(MAXDOC)
    doc_ends = jnp.cumsum(raw, axis=1)
    doc_begins = doc_ends - raw
    return jnp.clip(LEN - doc_begins, 0, raw).astype(jnp.int32)


def shard_levels(stream_key, dims, cuts, smallest, high):
    def one(dim, parts):
        steps = jax.random.uniform(jax.random.fold_in(jax.random.fold_in(stream_key, 6), dim), (parts,), jnp.float32, smallest / len(cuts), high / len(cuts))
        return jnp.repeat(jnp.exp(steps), dims[dim] // parts).reshape((-1,) + (1,) * (len(dims) - dim - 1))

    gain = one(*cuts[0])
    for cut in cuts[1:]:
        gain = gain * one(*cut)
    return gain


def gaussian(stream_key, shape, width, bound, cuts=(), kind=jnp.bfloat16):
    factor_of = shard_levels(stream_key, shape, cuts, -0.22, 0.18) if cuts else 1.0
    entries = jax.random.normal(stream_key, shape, jnp.float32) * width * factor_of
    return jnp.minimum(jnp.maximum(entries, -bound), bound).astype(kind)


def setup_inputs(seed: int = 0) -> dict:
    streams_of = jax.random.split(jax.random.key(seed), 5)
    queries = draw_queries(jax.random.fold_in(streams_of[4], 71), 0)
    keys = draw_keys(jax.random.fold_in(streams_of[4], 71), 0)
    values = gaussian(streams_of[2], (SEQS, LEN, KVH * HD), 1.0, 6.0, ((0, 2), (1, 16)))
    doc_lengths = draw_doc_lengths(jax.random.fold_in(streams_of[4], 71), 0)
    return dict(queries=queries, keys=keys, values=values, doc_lengths=doc_lengths)


def doc_starts(lengths_row, positions):
    doc_ends = jnp.cumsum(lengths_row).astype(jnp.int32)
    return lax.optimization_barrier(jnp.max(jnp.where(doc_ends[None, :] <= positions[:, None], doc_ends, 0), axis=1)).astype(jnp.int32)

def one_sequence(operands):
    seq_queries, seq_keys, seq_values, lengths_row = operands
    block_rows = min(512, LEN)
    window = MAXDOC + block_rows
    score_scale = 1.0 / math.sqrt(HD)
    grouped = seq_queries.reshape(LEN, KVH, GROUP, HD)
    padded_keys = jnp.concatenate([jnp.zeros((MAXDOC, KVH * HD), seq_keys.dtype), seq_keys], axis=0).reshape(MAXDOC + LEN, KVH, HD)
    padded_values = jnp.concatenate([jnp.zeros((MAXDOC, KVH * HD), seq_values.dtype), seq_values], axis=0).reshape(MAXDOC + LEN, KVH, HD)

    def one_block(block_index):
        first_row = (block_index * block_rows).astype(jnp.int32)
        query_block = lax.dynamic_slice_in_dim(grouped, first_row, block_rows, 0).astype(jnp.float32)
        key_window = lax.dynamic_slice_in_dim(padded_keys, first_row, window, 0).astype(jnp.float32)
        value_window = lax.dynamic_slice_in_dim(padded_values, first_row, window, 0).astype(jnp.float32)
        positions = first_row + jnp.arange(block_rows, dtype=jnp.int32)
        key_positions = first_row - MAXDOC + jnp.arange(window, dtype=jnp.int32)
        starts = doc_starts(lengths_row, positions)
        allowed = (key_positions[None, :] >= starts[:, None]) & (key_positions[None, :] <= positions[:, None])
        scores = jnp.einsum('qkgd,tkd->kgqt', query_block, key_window, precision=lax.Precision.HIGHEST) * score_scale
        masked = jnp.where(allowed[None, None], scores, -jnp.inf)
        peak = lax.optimization_barrier(jnp.max(masked, axis=-1, keepdims=True))
        weights = jnp.where(allowed[None, None], jnp.exp(scores - peak), 0.0).astype(jnp.bfloat16)
        weights_wide = weights.astype(jnp.float32)
        total = lax.optimization_barrier(jnp.sum(weights_wide, axis=-1))
        summed = jnp.einsum('kgqt,tkd->qkgd', weights_wide, value_window, precision=lax.Precision.HIGHEST)
        result = summed / jnp.transpose(total, (2, 0, 1))[..., None]
        return result.astype(jnp.bfloat16).reshape(block_rows, QH * HD)
    blocks = lax.map(one_block, jnp.arange(LEN // block_rows, dtype=jnp.int32))
    return blocks.reshape(LEN, QH * HD)

def reference(queries, keys, values, doc_lengths):
    return lax.map(one_sequence, (queries, keys, values, doc_lengths))
```

```python
import functools
import math

import jax
import jax.numpy as jnp
from jax import lax
from jax.experimental import pallas as pl
from jax.experimental.pallas import tpu as pltpu
from jax.sharding import PartitionSpec as P

QH = 64
KVH = 8
HD = 128
GROUP = 8
MASKED = -1e30


def doc_starts(lengths_row, positions):
    doc_ends = jnp.cumsum(lengths_row)
    return jnp.max(jnp.where(doc_ends[None, :] <= positions[:, None], doc_ends, 0), axis=1)


def attend(first_row, rows, blocks, bases, first_position, starts, q, kv, bias, out):
    tokens = kv.shape[1]
    exponent_scale = math.log2(math.e) / math.sqrt(HD)
    span = slice(first_row, first_row + rows)
    width = tokens * len(blocks)
    row_position = (
        first_position + first_row + lax.broadcasted_iota(jnp.int32, (rows, tokens), 0)
    )
    column = lax.broadcasted_iota(jnp.int32, (rows, tokens), 1)
    begin = starts[span, :tokens]
    for slot, base in enumerate(bases):
        key_position = base + column
        allowed = (key_position >= begin) & (key_position <= row_position)
        bias[span, slot * tokens : (slot + 1) * tokens] = jnp.where(allowed, 0.0, MASKED)
    mask = bias[span, :width]
    wide_mask = jnp.concatenate([mask] * GROUP, axis=0)
    ones = jnp.ones((width, HD), jnp.bfloat16)
    for g in range(KVH):
        columns = slice(g * HD, (g + 1) * HD)
        value_columns = slice((KVH + g) * HD, (KVH + g + 1) * HD)
        q_rows = jnp.concatenate(
            [q[span, (g * GROUP + h) * HD : (g * GROUP + h + 1) * HD] for h in range(GROUP)],
            axis=0,
        )
        k = jnp.concatenate([kv[b, :, columns] for b in blocks], axis=0)
        v = jnp.concatenate([kv[b, :, value_columns] for b in blocks], axis=0)
        v = jnp.concatenate([v, ones], axis=1)
        scores = (
            lax.dot_general(q_rows, k, (((1,), (1,)), ((), ())), preferred_element_type=jnp.float32)
            + wide_mask
        )
        peak = jnp.max(scores, axis=1, keepdims=True)
        weights = jnp.exp2((scores - peak) * exponent_scale).astype(jnp.bfloat16)
        summed = jnp.dot(weights, v, preferred_element_type=jnp.float32)
        result = (summed[:, :HD] / summed[:, HD:]).astype(jnp.bfloat16)
        for h in range(GROUP):
            out[span, (g * GROUP + h) * HD : (g * GROUP + h + 1) * HD] = result[
                h * rows : (h + 1) * rows
            ]


def attention_kernel(group, near, far, *refs):
    pairs = 1 + len(near) + len(far)
    starts, q_hbm = refs[:2]
    kv_hbm = refs[2 : 2 + 2 * pairs]
    out_hbm = refs[2 + 2 * pairs]
    q, kv, bias, out, sems = refs[3 + 2 * pairs :]
    tokens = q.shape[0]
    copies = [pltpu.make_async_copy(q_hbm, q, sems.at[2 * pairs])]
    copies += [
        pltpu.make_async_copy(kv_hbm[b], kv.at[b], sems.at[b]) for b in range(2 * pairs)
    ]
    for copy in copies:
        copy.start()
    for copy in copies:
        copy.wait()
    index = lax.axis_index("seq")
    pair, core = index // 2, index % 2
    first_position = index * tokens
    never = jnp.int32(1 << 30)

    def base_of(distance, valid):
        source = (pair - distance) * 2
        return [
            jnp.where(valid, (source + core) * tokens, never),
            jnp.where(valid, (source + 1 - core) * tokens, never),
        ]

    lowest = jnp.where(pair <= group, 0, group)
    within = functools.partial(
        attend, first_position=first_position, starts=starts, q=q, kv=kv, bias=bias, out=out
    )

    @pl.when(pair != group)
    def _():
        bases = base_of(0, True)
        for d in near:
            bases += base_of(d, pair - d >= lowest)
        within(0, tokens, range(2 * (1 + len(near))), bases)

    @pl.when(pair == group)
    def _():
        blocks, bases = [0, 1], base_of(0, True)
        for slot, d in enumerate(near):
            if d <= group // 2:
                blocks += [2 + 2 * slot, 3 + 2 * slot]
                bases += base_of(d, True)
        for slot, d in enumerate(far):
            blocks += [2 + 2 * len(near) + 2 * slot, 3 + 2 * len(near) + 2 * slot]
            bases += base_of(d, True)
        within(0, tokens // 2, blocks, bases)
        within(tokens // 2, tokens // 2, [0, 1], base_of(0, True))

    copy = pltpu.make_async_copy(out, out_hbm, sems.at[2 * pairs])
    copy.start()
    copy.wait()


def per_device(queries, keys, values, doc_lengths):
    tokens = queries.shape[1]
    seq_count = lax.axis_size("seq")
    pairs = seq_count // 2
    group = pairs // 2
    half = group // 2
    index = lax.axis_index("seq")

    def send(block, routes):
        devices = [(2 * a + core, 2 * b + core) for a, b in routes for core in (0, 1)]
        return lax.ppermute(block, "seq", devices)

    def swap(block):
        return lax.ppermute(block, "seq", [(i, i ^ 1) for i in range(seq_count)])

    own = jnp.concatenate([keys[0], values[0]], axis=1)
    near = [half] + [d for d in range(1, group) if d != half]
    far = list(range(half + 1, group + 1))
    received = {}
    for d in near:
        routes = [(p - d, p) for p in range(d, group)]
        routes += [(p - d, p) for p in range(group + d, pairs)]
        if d <= half:
            routes.append((group - d, group))
        received[d] = send(own, routes)
    passed = [send(received[half], [(group - d + half, group)]) for d in far]
    blocks = []
    for block in [own] + [received[d] for d in near] + passed:
        blocks += [block, swap(block)]
    lengths_row = lax.dynamic_index_in_dim(doc_lengths, lax.axis_index("dp"), 0, keepdims=False)
    positions = index * tokens + jnp.arange(tokens, dtype=jnp.int32)
    starts = jnp.broadcast_to(doc_starts(lengths_row, positions)[:, None], (tokens, 128))
    any_spec = pl.BlockSpec(memory_space=pl.ANY)
    out = pl.pallas_call(
        functools.partial(attention_kernel, group, near, far),
        out_shape=jax.ShapeDtypeStruct((tokens, QH * HD), jnp.bfloat16),
        in_specs=[pl.BlockSpec(memory_space=pltpu.VMEM)] + [any_spec] * (1 + len(blocks)),
        out_specs=any_spec,
        scratch_shapes=[
            pltpu.VMEM((tokens, QH * HD), jnp.bfloat16),
            pltpu.VMEM((len(blocks), tokens, 2 * KVH * HD), jnp.bfloat16),
            pltpu.VMEM((tokens, tokens * len(blocks)), jnp.float32),
            pltpu.VMEM((tokens, QH * HD), jnp.bfloat16),
            pltpu.SemaphoreType.DMA((len(blocks) + 1,)),
        ],
        compiler_params=pltpu.CompilerParams(vmem_limit_bytes=48 * 1024 * 1024),
    )(starts, queries[0], *blocks)
    return out[None]


def solution(mesh):
    placed = (P("dp", "seq", None), P("dp", "seq", None), P("dp", "seq", None), P())
    return jax.shard_map(
        per_device, mesh=mesh, in_specs=placed, out_specs=P("dp", "seq", None), check_vma=False
    )
```

```python
import functools
import math

import jax
import jax.numpy as jnp
from jax import lax
from jax.experimental import pallas as pl
from jax.experimental.pallas import tpu as pltpu
from jax.sharding import PartitionSpec as P

QH = 64
KVH = 8
HD = 128
GROUP = 8
WIDE = GROUP * HD
MASKED = -1e30
EXPONENT_SCALE = math.log2(math.e) / math.sqrt(HD)
LOW_TOTAL, HIGH_TOTAL = 2.0**-60, 2.0**80
VMEM_LIMIT = 24 * 1024 * 1024


def join_kernel(keys, values, joined, sems):
    copies = [
        pltpu.make_async_copy(keys, joined.at[:, : KVH * HD], sems.at[0]),
        pltpu.make_async_copy(values, joined.at[:, KVH * HD :], sems.at[1]),
    ]
    for copy in copies:
        copy.start()
    for copy in copies:
        copy.wait()


def doc_starts(lengths_row, positions):
    doc_ends = jnp.cumsum(lengths_row)
    return jnp.max(jnp.where(doc_ends[None, :] <= positions[:, None], doc_ends, 0), axis=1)


def columns(first, width=HD):
    return pl.ds(first if isinstance(first, int) else pl.multiple_of(first, HD), width)


def mask_of(first, rows, tokens, bases, first_position, starts):
    row_position = first_position + first + lax.broadcasted_iota(jnp.int32, (rows, tokens), 0)
    column = lax.broadcasted_iota(jnp.int32, (rows, tokens), 1)
    begin = starts[first : first + rows, :tokens]
    parts = []
    for base in bases:
        key_position = base + column
        allowed = (key_position >= begin) & (key_position <= row_position)
        parts.append(jnp.where(allowed, 0.0, MASKED))
    return jnp.concatenate(parts, axis=1)


def exponents_of(g, first, rows, q, blocks, mask):
    q_rows = jnp.concatenate(
        [q[first : first + rows, columns((g * GROUP + h) * HD)] for h in range(GROUP)], axis=0
    )
    k = jnp.concatenate([b[:, columns(g * HD)] for b in blocks], axis=0)
    scores = lax.dot_general(
        q_rows, k, (((1,), (1,)), ((), ())), preferred_element_type=jnp.float32
    )
    masked = scores.reshape(GROUP, rows, -1) + mask[None]
    return masked.reshape(scores.shape) * EXPONENT_SCALE


def weighted_sum(g, exponents, blocks):
    v = jnp.concatenate([b[:, columns((KVH + g) * HD)] for b in blocks], axis=0)
    v = jnp.concatenate([v, jnp.ones_like(v)], axis=1)
    weights = jnp.exp2(exponents).astype(jnp.bfloat16)
    return jnp.dot(weights, v, preferred_element_type=jnp.float32)


def load_kernel(source, target, sem):
    copy = pltpu.make_async_copy(source, target, sem)
    copy.start()
    copy.wait()


def early_kernel(base_of, q, starts, *refs):
    blocks, summed = refs[:-1], refs[-1]
    tokens = q.shape[0]
    index = lax.axis_index("seq")
    mask = mask_of(0, tokens, tokens, base_of(index, tokens), index * tokens, starts)
    for g in range(KVH):
        summed[g] = weighted_sum(g, exponents_of(g, 0, tokens, q, blocks, mask), blocks)


def late_kernel(group, base_of, late_base_of, q, starts, summed, early, high, middle, out_hbm, out, sems):
    tokens = q.shape[0]
    index = lax.axis_index("seq")
    early_bases = base_of(index, tokens)
    at_high, at_middle = late_base_of(index, tokens)

    def store(g, first, rows, total):
        result = (total[:, :HD] / total[:, HD:]).astype(jnp.bfloat16)
        for h in range(GROUP):
            out[first : first + rows, columns((g * GROUP + h) * HD)] = result[
                h * rows : (h + 1) * rows
            ]

    def copy_of(g):
        part = columns(g * WIDE, WIDE)
        return pltpu.make_async_copy(out.at[:, part], out_hbm.at[:, part], sems.at[g])

    def earlier(g, first, rows):
        return jnp.concatenate(
            [summed[g, h * tokens + first : h * tokens + first + rows] for h in range(GROUP)],
            axis=0,
        )

    def shifted(first, rows, blocks, bases):
        mask = mask_of(first, rows, tokens, bases, index * tokens, starts)

        def one(g, _):
            exponents = exponents_of(g, first, rows, q, blocks, mask)
            peak = jnp.max(exponents, axis=1, keepdims=True)
            store(g, first, rows, weighted_sum(g, exponents - peak, blocks))
            return 0

        lax.fori_loop(0, KVH, one, 0)

    def finish(rows, blocks, bases):
        mask = mask_of(0, rows, tokens, bases, index * tokens, starts)
        faults = jnp.zeros((GROUP * tokens, HD), jnp.float32)
        for g in range(KVH):
            new = weighted_sum(g, exponents_of(g, 0, rows, q, blocks, mask), blocks)
            totals = [earlier(g, 0, rows) + new]
            if rows < tokens:
                totals.append(earlier(g, rows, tokens - rows))
            for first, total in zip((0, rows), totals):
                store(g, first, total.shape[0] // GROUP, total)
            weights = jnp.concatenate([total[:, HD:] for total in totals], axis=0)
            sound = (weights > LOW_TOTAL) & (weights < HIGH_TOTAL)
            faults = jnp.maximum(faults, jnp.where(sound, 0.0, 1.0))
            copy_of(g).start()
        any_fault = jnp.max(faults) > 0.0
        for g in range(KVH):
            copy_of(g).wait()

        @pl.when(any_fault)
        def _():
            shifted(0, rows, early + blocks, early_bases + bases)
            if rows < tokens:
                shifted(rows, tokens - rows, early, early_bases)
            for g in range(KVH):
                copy_of(g).start()
            for g in range(KVH):
                copy_of(g).wait()

    is_middle = index // 2 == group
    pl.when(~is_middle)(functools.partial(finish, tokens, high, at_high))
    pl.when(is_middle)(functools.partial(finish, tokens // 2, middle, at_middle))


def closed(routes, count):
    onward = dict(routes)
    backward = {b: a for a, b in routes}
    for device in range(count):
        sibling = device ^ 1
        if device not in onward and device not in backward and sibling not in backward:
            onward[device], backward[sibling] = sibling, device
    for device in range(count):
        if device not in onward:
            start = device
            while start in backward:
                start = backward[start]
            onward[device], backward[start] = start, device
    return sorted(onward.items())


def per_device(queries, keys, values, doc_lengths):
    tokens = queries.shape[1]
    seq_count = lax.axis_size("seq")
    pairs = seq_count // 2
    group = pairs // 2
    half = group // 2
    never = 1 << 30

    def send(block, routes):
        devices = [(2 * a + i, 2 * b + j) for a, i, b, j in routes]
        return lax.ppermute(block, "seq", closed(devices, seq_count))

    def swap(block):
        return lax.ppermute(block, "seq", [(2 * c + i, 2 * c + 1 - i) for c in range(pairs) for i in (0, 1)])

    any_spec = pl.BlockSpec(memory_space=pl.ANY)
    vmem_spec = pl.BlockSpec(memory_space=pltpu.VMEM)
    params = pltpu.CompilerParams(vmem_limit_bytes=VMEM_LIMIT)

    def in_hbm(array):
        return pltpu.with_memory_space_constraint(array, pltpu.HBM)

    def resident(array):
        return pltpu.with_memory_space_constraint(array, pltpu.VMEM)

    own = pl.pallas_call(
        join_kernel,
        out_shape=pltpu.VMEM((tokens, 2 * KVH * HD), jnp.bfloat16),
        in_specs=[any_spec] * 2,
        out_specs=vmem_spec,
        scratch_shapes=[pltpu.SemaphoreType.DMA((2,))],
        compiler_params=params,
    )(in_hbm(keys[0]), in_hbm(values[0]))

    halves = [(first, first + half) for first in range(0, pairs, half)]
    up = [(c, c + half) for c in [*range(half + 1), *range(group, group + half)]]
    along = {
        d: [(c - d, c) for lo, hi in halves for c in range(lo + d, hi)] + [(group - d, group)]
        for d in range(1, half)
    }
    routes = {half: up, **along}
    ordered = [half, *along]
    distances = [ordered, [ordered[1], half, *ordered[2:]]]
    up_round = [0, 1]
    first = []
    for of_zero, of_one in zip(*distances):
        both = ((0, of_zero), (1, of_one))
        first.append(send(own, [(a, core, b, core) for core, d in both for a, b in routes[d]]))
    sibling = swap(own)
    own_later, _ = lax.optimization_barrier((own, first[1]))
    cross = [
        send(
            own_later,
            [
                (lo + (j - step) % half, core, lo + half + j, core)
                for lo in (0, group)
                for j in range(half)
                for core in (0, 1)
            ]
            + [
                (lo + half + j, core, lo + j, core)
                for lo in (0, group)
                for j in range(half)
                for core in (0, 1)
            ],
        )
        for step in range(1, half)
    ]
    far, far_blocks = [], []
    for low in range(0, half, 2):
        for core in (0, 1):
            one, two, other = half + low, half + low + 1, 1 - core
            passed = [(one, core, group, 0), (group, 0, one, other), (one, other, one, core)]
            passed += [(two, core, group, 1), (group, 1, group + 1, 0)]
            passed += [(group + 1, 0, group + 1, 1), (group + 1, 1, two, other)]
            passed += [(two, other, two, core)]
            far.append(send(first[up_round[core]], passed))
            far_blocks.append((low, core))

    def position(source, core, tokens, valid):
        return jnp.where(valid, (2 * source + core) * tokens, never)

    def early_bases(index, tokens):
        pair, core = index // 2, index % 2
        bases = [position(pair, core, tokens, True), position(pair, 1 - core, tokens, True)]
        for of_zero, of_one in zip(*distances):
            for other in (core, 1 - core):
                d = jnp.where(other == 0, of_zero, of_one)
                high = pair // half % 2 == 1
                valid = jnp.where(d == half, high, pair % half >= d) | (pair == group)
                bases.append(position(pair - d, other, tokens, valid))
        return bases

    def late_bases(index, tokens):
        pair, core = index // 2, index % 2
        local = pair % half
        at_high, at_middle = [], []
        for step in range(1, half):
            source = pair - half - local + (local + half - step) % half
            for other in (core, 1 - core):
                at_high.append(position(source, other, tokens, pair // half % 2 == 1))
        for low, other in far_blocks:
            at_middle.append(position(low + core, other, tokens, True))
            at_middle.append(position(low + 1 - core, other, tokens, True))
        return at_high, at_middle

    lengths_row = lax.dynamic_index_in_dim(doc_lengths, lax.axis_index("dp"), 0, keepdims=False)
    positions = lax.axis_index("seq") * tokens + jnp.arange(tokens, dtype=jnp.int32)
    starts = jnp.broadcast_to(doc_starts(lengths_row, positions)[:, None], (tokens, HD))
    early = [own, sibling]
    for block in first:
        early += [block, swap(block)]
    early = [resident(a) for a in early]
    q = pl.pallas_call(
        load_kernel,
        out_shape=pltpu.VMEM((tokens, QH * HD), jnp.bfloat16),
        in_specs=[any_spec],
        out_specs=vmem_spec,
        scratch_shapes=[pltpu.SemaphoreType.DMA(())],
        compiler_params=params,
    )(in_hbm(queries[0]))
    summed = pl.pallas_call(
        functools.partial(early_kernel, early_bases),
        out_shape=pltpu.VMEM((KVH, GROUP * tokens, 2 * HD), jnp.float32),
        in_specs=[vmem_spec] * (2 + len(early)),
        out_specs=vmem_spec,
        compiler_params=params,
        cost_estimate=pl.CostEstimate(flops=1, bytes_accessed=1, transcendentals=0),
    )(resident(q), resident(starts), *early)

    late = []
    for blocks in (cross, far):
        held = []
        for block in blocks:
            block, summed = lax.optimization_barrier((block, summed))
            held += [block, swap(block)]
        late.append([resident(a) for a in held])
    out = pl.pallas_call(
        functools.partial(late_kernel, group, early_bases, late_bases),
        out_shape=jax.ShapeDtypeStruct((tokens, QH * HD), jnp.bfloat16),
        in_specs=[vmem_spec] * 3 + [[vmem_spec] * len(a) for a in (early, *late)],
        out_specs=any_spec,
        scratch_shapes=[
            pltpu.VMEM((tokens, QH * HD), jnp.bfloat16),
            pltpu.SemaphoreType.DMA((KVH,)),
        ],
        compiler_params=params,
    )(resident(q), resident(starts), resident(summed), early, *late)
    return out[None]


def solution(mesh):
    placed = (P("dp", "seq", None), P("dp", "seq", None), P("dp", "seq", None), P())
    return jax.shard_map(
        per_device, mesh=mesh, in_specs=placed, out_specs=P("dp", "seq", None), check_vma=False
    )
```

```python
import functools
import math

import jax
import jax.numpy as jnp
from jax import lax
from jax.experimental import pallas as pl
from jax.experimental.pallas import tpu as pltpu
from jax.sharding import PartitionSpec as P

QH = 64
KVH = 8
HD = 128
GROUP = 8
WIDE = GROUP * HD
MASKED = -1e30
EXPONENT_SCALE = math.log2(math.e) / math.sqrt(HD)
LOW_TOTAL, HIGH_TOTAL = 2.0**-60, 2.0**80
VMEM_LIMIT = 24 * 1024 * 1024


def join_kernel(keys, values, joined, sems):
    copies = [
        pltpu.make_async_copy(keys, joined.at[:, : KVH * HD], sems.at[0]),
        pltpu.make_async_copy(values, joined.at[:, KVH * HD :], sems.at[1]),
    ]
    for copy in copies:
        copy.start()
    for copy in copies:
        copy.wait()


def doc_starts(lengths_row, positions):
    doc_ends = jnp.cumsum(lengths_row)
    return jnp.max(jnp.where(doc_ends[None, :] <= positions[:, None], doc_ends, 0), axis=1)


def columns(first, width=HD):
    return pl.ds(first if isinstance(first, int) else pl.multiple_of(first, HD), width)


def mask_of(first, rows, tokens, bases, first_position, starts):
    row_position = first_position + first + lax.broadcasted_iota(jnp.int32, (rows, tokens), 0)
    column = lax.broadcasted_iota(jnp.int32, (rows, tokens), 1)
    begin = starts[first : first + rows, :tokens]
    parts = []
    for base in bases:
        key_position = base + column
        allowed = (key_position >= begin) & (key_position <= row_position)
        parts.append(jnp.where(allowed, 0.0, MASKED))
    return jnp.concatenate(parts, axis=1)


def exponents_of(g, first, rows, q, blocks, mask):
    q_rows = jnp.concatenate(
        [q[first : first + rows, columns((g * GROUP + h) * HD)] for h in range(GROUP)], axis=0
    )
    k = jnp.concatenate([b[:, columns(g * HD)] for b in blocks], axis=0)
    scores = lax.dot_general(
        q_rows, k, (((1,), (1,)), ((), ())), preferred_element_type=jnp.float32
    )
    masked = scores.reshape(GROUP, rows, -1) + mask[None]
    return masked.reshape(scores.shape) * EXPONENT_SCALE


def weighted_sum(g, exponents, blocks):
    v = jnp.concatenate([b[:, columns((KVH + g) * HD)] for b in blocks], axis=0)
    v = jnp.concatenate([v, jnp.ones_like(v)], axis=1)
    weights = jnp.exp2(exponents).astype(jnp.bfloat16)
    return jnp.dot(weights, v, preferred_element_type=jnp.float32)


def load_kernel(source, target, sem):
    copy = pltpu.make_async_copy(source, target, sem)
    copy.start()
    copy.wait()


def copy_out(g, out, out_hbm, sems):
    part = columns(g * WIDE, WIDE)
    return pltpu.make_async_copy(out.at[:, part], out_hbm.at[:, part], sems.at[g])


def store(g, first, total, out):
    rows = total.shape[0] // GROUP
    result = (total[:, :HD] / total[:, HD:]).astype(jnp.bfloat16)
    for h in range(GROUP):
        out[first : first + rows, columns((g * GROUP + h) * HD)] = result[h * rows : (h + 1) * rows]


def finish(totals_of, spans, q, starts, first_position, out, out_hbm, sems):
    tokens = q.shape[0]
    faults = jnp.zeros((GROUP * tokens, HD), jnp.float32)
    for g in range(KVH):
        totals = totals_of(g)
        for (first, *_), total in zip(spans, totals):
            store(g, first, total, out)
        weights = jnp.concatenate([total[:, HD:] for total in totals], axis=0)
        sound = (weights > LOW_TOTAL) & (weights < HIGH_TOTAL)
        faults = jnp.maximum(faults, jnp.where(sound, 0.0, 1.0))
        copy_out(g, out, out_hbm, sems).start()
    any_fault = jnp.max(faults) > 0.0
    for g in range(KVH):
        copy_out(g, out, out_hbm, sems).wait()

    @pl.when(any_fault)
    def _():
        for first, rows, blocks, bases in spans:
            mask = mask_of(first, rows, tokens, bases, first_position, starts)

            def one(g, _):
                exponents = exponents_of(g, first, rows, q, blocks, mask)
                peak = jnp.max(exponents, axis=1, keepdims=True)
                store(g, first, weighted_sum(g, exponents - peak, blocks), out)
                return 0

            lax.fori_loop(0, KVH, one, 0)
        for g in range(KVH):
            copy_out(g, out, out_hbm, sems).start()
        for g in range(KVH):
            copy_out(g, out, out_hbm, sems).wait()


def early_kernel(group, half, base_of, q, starts, *refs):
    blocks, (summed, out_hbm, out, sems) = refs[:-4], refs[-4:]
    tokens = q.shape[0]
    index = lax.axis_index("seq")
    bases = base_of(index, tokens)
    mask = mask_of(0, tokens, tokens, bases, index * tokens, starts)
    for g in range(KVH):
        summed[g] = weighted_sum(g, exponents_of(g, 0, tokens, q, blocks, mask), blocks)
    pair = index // 2

    @pl.when((pair != group) & (pair // half % 2 == 0))
    def _():
        spans = [(0, tokens, blocks, bases)]
        finish(lambda g: [summed[g]], spans, q, starts, index * tokens, out, out_hbm, sems)


def late_kernel(
    reads, rows, base_of, late_base_of, q, starts, summed, early, late, _, out_hbm, out, sems
):
    tokens = q.shape[0]
    index = lax.axis_index("seq")

    def earlier(g, first, length):
        return jnp.concatenate(
            [summed[g, h * tokens + first : h * tokens + first + length] for h in range(GROUP)],
            axis=0,
        )

    @pl.when(reads(index // 2))
    def _():
        early_bases, bases = base_of(index, tokens), late_base_of(index, tokens)
        mask = mask_of(0, rows, tokens, bases, index * tokens, starts)
        exponents = [exponents_of(g, 0, rows, q, late, mask) for g in range(KVH)]
        new = [weighted_sum(g, exponents[g], late) for g in range(KVH)]
        spans = [(0, rows, early + late, early_bases + bases)]
        if rows < tokens:
            spans.append((rows, tokens - rows, early, early_bases))

        def totals_of(g):
            rest = [earlier(g, first, length) for first, length, *_ in spans[1:]]
            return [earlier(g, 0, rows) + new[g], *rest]

        finish(totals_of, spans, q, starts, index * tokens, out, out_hbm, sems)


def closed(routes, count):
    onward = dict(routes)
    backward = {b: a for a, b in routes}
    for device in range(count):
        sibling = device ^ 1
        if device not in onward and device not in backward and sibling not in backward:
            onward[device], backward[sibling] = sibling, device
    for device in range(count):
        if device not in onward:
            start = device
            while start in backward:
                start = backward[start]
            onward[device], backward[start] = start, device
    return sorted(onward.items())


def per_device(queries, keys, values, doc_lengths):
    tokens = queries.shape[1]
    seq_count = lax.axis_size("seq")
    pairs = seq_count // 2
    group = pairs // 2
    half = group // 2
    never = 1 << 30

    def send(block, routes):
        devices = [(2 * a + i, 2 * b + j) for a, i, b, j in routes]
        return lax.ppermute(block, "seq", closed(devices, seq_count))

    def swap(block):
        return lax.ppermute(block, "seq", [(2 * c + i, 2 * c + 1 - i) for c in range(pairs) for i in (0, 1)])

    any_spec = pl.BlockSpec(memory_space=pl.ANY)
    vmem_spec = pl.BlockSpec(memory_space=pltpu.VMEM)
    params = pltpu.CompilerParams(vmem_limit_bytes=VMEM_LIMIT)

    def in_hbm(array):
        return pltpu.with_memory_space_constraint(array, pltpu.HBM)

    def resident(array):
        return pltpu.with_memory_space_constraint(array, pltpu.VMEM)

    own = pl.pallas_call(
        join_kernel,
        out_shape=pltpu.VMEM((tokens, 2 * KVH * HD), jnp.bfloat16),
        in_specs=[any_spec] * 2,
        out_specs=vmem_spec,
        scratch_shapes=[pltpu.SemaphoreType.DMA((2,))],
        compiler_params=params,
    )(in_hbm(keys[0]), in_hbm(values[0]))

    halves = [(first, first + half) for first in range(0, pairs, half)]
    up = [(c, c + half) for c in [*range(half + 1), *range(group, group + half)]]
    along = {
        d: [(c - d, c) for lo, hi in halves for c in range(lo + d, hi)] + [(group - d, group)]
        for d in range(1, half)
    }
    routes = {half: up, **along}
    distances = [half, *along]
    sibling = swap(own)
    own_next, _ = lax.optimization_barrier((own, sibling))
    first = [
        send(
            own if d == half else own_next,
            [(a, core, b, core) for a, b in routes[d] for core in (0, 1)],
        )
        for d in distances
    ]
    swapped = [swap(block) for block in first]
    q = pl.pallas_call(
        load_kernel,
        out_shape=pltpu.VMEM((tokens, QH * HD), jnp.bfloat16),
        in_specs=[any_spec],
        out_specs=vmem_spec,
        scratch_shapes=[pltpu.SemaphoreType.DMA(())],
        compiler_params=params,
    )(in_hbm(queries[0]))
    first[0], q = lax.optimization_barrier((first[0], q))
    own_later, _ = lax.optimization_barrier((own, first[0]))
    came_up = first[0]
    cross = [
        send(
            own_later,
            [
                (lo + (j - step) % half, core, lo + half + j, core)
                for lo in (0, group)
                for j in range(half)
                for core in (0, 1)
            ]
            + [
                (lo + half + j, core, lo + j, core)
                for lo in (0, group)
                for j in range(half)
                for core in (0, 1)
            ],
        )
        for step in range(1, half)
    ]
    far = []
    for j in range(half):
        back = [] if j % 2 == 0 else [group + 1]
        route = [half + j, group, *back, half + j]
        far.append(
            send(came_up, [(a, c, b, c) for a, b in zip(route, route[1:]) for c in (0, 1)])
        )

    def position(source, core, tokens, valid):
        return jnp.where(valid, (2 * source + core) * tokens, never)

    def early_bases(index, tokens):
        pair, core = index // 2, index % 2
        bases = [position(pair, core, tokens, True), position(pair, 1 - core, tokens, True)]
        for d in distances:
            reached = pair // half % 2 == 1 if d == half else pair % half >= d
            for other in (core, 1 - core):
                bases.append(position(pair - d, other, tokens, reached | (pair == group)))
        return bases

    def high_bases(index, tokens):
        pair, core = index // 2, index % 2
        local = pair % half
        bases = []
        for step in range(1, half):
            source = pair - half - local + (local + half - step) % half
            bases += [position(source, other, tokens, True) for other in (core, 1 - core)]
        return bases

    def middle_bases(index, tokens):
        core = index % 2
        return [
            position(low, other, tokens, True) for low in range(half) for other in (core, 1 - core)
        ]

    lengths_row = lax.dynamic_index_in_dim(doc_lengths, lax.axis_index("dp"), 0, keepdims=False)
    positions = lax.axis_index("seq") * tokens + jnp.arange(tokens, dtype=jnp.int32)
    starts = jnp.broadcast_to(doc_starts(lengths_row, positions)[:, None], (tokens, HD))
    early = [own, sibling]
    for block, other in zip(first, swapped):
        early += [block, other]
    early = [resident(a) for a in early]
    out_scratch = [pltpu.VMEM((tokens, QH * HD), jnp.bfloat16), pltpu.SemaphoreType.DMA((KVH,))]
    result = jax.ShapeDtypeStruct((tokens, QH * HD), jnp.bfloat16)
    summed, out = pl.pallas_call(
        functools.partial(early_kernel, group, half, early_bases),
        out_shape=[pltpu.VMEM((KVH, GROUP * tokens, 2 * HD), jnp.float32), result],
        in_specs=[vmem_spec] * (2 + len(early)),
        out_specs=[vmem_spec, any_spec],
        scratch_shapes=out_scratch,
        compiler_params=params,
        cost_estimate=pl.CostEstimate(flops=1, bytes_accessed=1, transcendentals=0),
    )(resident(q), resident(starts), *early)

    arrived = []
    for blocks in (far, cross):
        held = []
        for block in blocks:
            block, summed = lax.optimization_barrier((block, summed))
            held += [block, swap(block)]
        arrived.append([resident(a) for a in held])
    middle, high = arrived
    for reads, rows, bases, late in (
        (lambda pair: pair // half % 2 == 1, tokens, high_bases, high),
        (lambda pair: pair == group, tokens // 2, middle_bases, middle),
    ):
        out = pl.pallas_call(
            functools.partial(late_kernel, reads, rows, early_bases, bases),
            out_shape=result,
            in_specs=[vmem_spec] * 3 + [[vmem_spec] * len(a) for a in (early, late)] + [any_spec],
            out_specs=any_spec,
            scratch_shapes=out_scratch,
            input_output_aliases={3 + len(early) + len(late): 0},
            compiler_params=params,
            cost_estimate=pl.CostEstimate(flops=1, bytes_accessed=1, transcendentals=0),
        )(resident(q), resident(starts), resident(summed), early, late, out)
    return out[None]


def solution(mesh):
    placed = (P("dp", "seq", None), P("dp", "seq", None), P("dp", "seq", None), P())
    return jax.shard_map(
        per_device, mesh=mesh, in_specs=placed, out_specs=P("dp", "seq", None), check_vma=False
    )
```

```python
import functools
import math

import jax
import jax.numpy as jnp
from jax import lax
from jax.experimental import pallas as pl
from jax.experimental.pallas import tpu as pltpu
from jax.sharding import PartitionSpec as P

QH = 64
KVH = 8
HD = 128
GROUP = 8
WIDE = GROUP * HD
MASKED = -1e30
EXPONENT_SCALE = math.log2(math.e) / math.sqrt(HD)
LOW_TOTAL, HIGH_TOTAL = 2.0**-60, 2.0**80
VMEM_LIMIT = 24 * 1024 * 1024


def join_kernel(keys, values, joined, sems):
    copies = [
        pltpu.make_async_copy(keys, joined.at[:, : KVH * HD], sems.at[0]),
        pltpu.make_async_copy(values, joined.at[:, KVH * HD :], sems.at[1]),
    ]
    for copy in copies:
        copy.start()
    for copy in copies:
        copy.wait()


def doc_starts(lengths_row, positions):
    doc_ends = jnp.cumsum(lengths_row)
    return jnp.max(jnp.where(doc_ends[None, :] <= positions[:, None], doc_ends, 0), axis=1)


def columns(first, width=HD):
    return pl.ds(first if isinstance(first, int) else pl.multiple_of(first, HD), width)


def mask_of(first, rows, tokens, bases, first_position, starts):
    row_position = first_position + first + lax.broadcasted_iota(jnp.int32, (rows, tokens), 0)
    column = lax.broadcasted_iota(jnp.int32, (rows, tokens), 1)
    begin = starts[first : first + rows, :tokens]
    parts = []
    for base in bases:
        key_position = base + column
        allowed = (key_position >= begin) & (key_position <= row_position)
        parts.append(jnp.where(allowed, 0.0, MASKED))
    return jnp.concatenate(parts, axis=1)


def exponents_of(g, first, rows, q, blocks, mask):
    q_rows = jnp.concatenate(
        [q[first : first + rows, columns((g * GROUP + h) * HD)] for h in range(GROUP)], axis=0
    )
    k = jnp.concatenate([b[:, columns(g * HD)] for b in blocks], axis=0)
    scores = lax.dot_general(
        q_rows, k, (((1,), (1,)), ((), ())), preferred_element_type=jnp.float32
    )
    masked = scores.reshape(GROUP, rows, -1) + mask[None]
    return masked.reshape(scores.shape) * EXPONENT_SCALE


def weighted_sum(g, exponents, blocks):
    v = jnp.concatenate([b[:, columns((KVH + g) * HD)] for b in blocks], axis=0)
    v = jnp.concatenate([v, jnp.ones_like(v)], axis=1)
    weights = jnp.exp2(exponents).astype(jnp.bfloat16)
    return jnp.dot(weights, v, preferred_element_type=jnp.float32)


def load_kernel(source, target, sem):
    copy = pltpu.make_async_copy(source, target, sem)
    copy.start()
    copy.wait()


def copy_out(g, out, out_hbm, sems):
    part = columns(g * WIDE, WIDE)
    return pltpu.make_async_copy(out.at[:, part], out_hbm.at[:, part], sems.at[g])


def store(g, first, total, out):
    rows = total.shape[0] // GROUP
    result = (total[:, :HD] / total[:, HD:]).astype(jnp.bfloat16)
    for h in range(GROUP):
        out[first : first + rows, columns((g * GROUP + h) * HD)] = result[h * rows : (h + 1) * rows]


def finish(totals_of, spans, q, starts, first_position, out, out_hbm, sems):
    tokens = q.shape[0]
    faults = jnp.zeros((GROUP * tokens, HD), jnp.float32)
    for g in range(KVH):
        totals = totals_of(g)
        for (first, *_), total in zip(spans, totals):
            store(g, first, total, out)
        weights = jnp.concatenate([total[:, HD:] for total in totals], axis=0)
        sound = (weights > LOW_TOTAL) & (weights < HIGH_TOTAL)
        faults = jnp.maximum(faults, jnp.where(sound, 0.0, 1.0))
        copy_out(g, out, out_hbm, sems).start()
    any_fault = jnp.max(faults) > 0.0
    for g in range(KVH):
        copy_out(g, out, out_hbm, sems).wait()

    @pl.when(any_fault)
    def _():
        for first, rows, blocks, bases in spans:
            mask = mask_of(first, rows, tokens, bases, first_position, starts)

            def one(g, _):
                exponents = exponents_of(g, first, rows, q, blocks, mask)
                peak = jnp.max(exponents, axis=1, keepdims=True)
                store(g, first, weighted_sum(g, exponents - peak, blocks), out)
                return 0

            lax.fori_loop(0, KVH, one, 0)
        for g in range(KVH):
            copy_out(g, out, out_hbm, sems).start()
        for g in range(KVH):
            copy_out(g, out, out_hbm, sems).wait()


def early_kernel(group, half, base_of, q, starts, *refs):
    blocks, (summed, out_hbm, out, sems) = refs[:-4], refs[-4:]
    tokens = q.shape[0]
    index = lax.axis_index("seq")
    bases = base_of(index, tokens)
    mask = mask_of(0, tokens, tokens, bases, index * tokens, starts)
    for g in range(KVH):
        summed[g] = weighted_sum(g, exponents_of(g, 0, tokens, q, blocks, mask), blocks)
    pair = index // 2

    @pl.when((pair != group) & (pair // half % 2 == 0))
    def _():
        spans = [(0, tokens, blocks, bases)]
        finish(lambda g: [summed[g]], spans, q, starts, index * tokens, out, out_hbm, sems)


def late_kernel(
    reads, rows, base_of, late_base_of, q, starts, summed, early, late, _, out_hbm, out, sems
):
    tokens = q.shape[0]
    index = lax.axis_index("seq")

    def earlier(g, first, length):
        return jnp.concatenate(
            [summed[g, h * tokens + first : h * tokens + first + length] for h in range(GROUP)],
            axis=0,
        )

    @pl.when(reads(index // 2))
    def _():
        early_bases, bases = base_of(index, tokens), late_base_of(index, tokens)
        mask = mask_of(0, rows, tokens, bases, index * tokens, starts)
        exponents = [exponents_of(g, 0, rows, q, late, mask) for g in range(KVH)]
        new = [weighted_sum(g, exponents[g], late) for g in range(KVH)]
        spans = [(0, rows, early + late, early_bases + bases)]
        if rows < tokens:
            spans.append((rows, tokens - rows, early, early_bases))

        def totals_of(g):
            rest = [earlier(g, first, length) for first, length, *_ in spans[1:]]
            return [earlier(g, 0, rows) + new[g], *rest]

        finish(totals_of, spans, q, starts, index * tokens, out, out_hbm, sems)


def closed(routes, count):
    onward = dict(routes)
    backward = {b: a for a, b in routes}
    for device in range(count):
        sibling = device ^ 1
        if device not in onward and device not in backward and sibling not in backward:
            onward[device], backward[sibling] = sibling, device
    for device in range(count):
        if device not in onward:
            start = device
            while start in backward:
                start = backward[start]
            onward[device], backward[start] = start, device
    return sorted(onward.items())


def per_device(queries, keys, values, doc_lengths):
    tokens = queries.shape[1]
    seq_count = lax.axis_size("seq")
    pairs = seq_count // 2
    group = pairs // 2
    half = group // 2
    never = 1 << 30

    def send(block, routes):
        devices = [(2 * a + i, 2 * b + j) for a, i, b, j in routes]
        return lax.ppermute(block, "seq", closed(devices, seq_count))

    def swap(block):
        return lax.ppermute(block, "seq", [(2 * c + i, 2 * c + 1 - i) for c in range(pairs) for i in (0, 1)])

    any_spec = pl.BlockSpec(memory_space=pl.ANY)
    vmem_spec = pl.BlockSpec(memory_space=pltpu.VMEM)
    params = pltpu.CompilerParams(vmem_limit_bytes=VMEM_LIMIT)

    def in_hbm(array):
        return pltpu.with_memory_space_constraint(array, pltpu.HBM)

    def resident(array):
        return pltpu.with_memory_space_constraint(array, pltpu.VMEM)

    own = pl.pallas_call(
        join_kernel,
        out_shape=pltpu.VMEM((tokens, 2 * KVH * HD), jnp.bfloat16),
        in_specs=[any_spec] * 2,
        out_specs=vmem_spec,
        scratch_shapes=[pltpu.SemaphoreType.DMA((2,))],
        compiler_params=params,
    )(in_hbm(keys[0]), in_hbm(values[0]))

    halves = [(first, first + half) for first in range(0, pairs, half)]
    up = [(c, c + half) for c in [*range(half + 1), *range(group, group + half)]]
    along = {
        d: [(c - d, c) for lo, hi in halves for c in range(lo + d, hi)] + [(group - d, group)]
        for d in range(1, half)
    }
    routes = {half: up, **along}
    distances = [half, *along]
    sibling = swap(own)
    own_next, _ = lax.optimization_barrier((own, sibling))
    first = [
        send(
            own if d == half else own_next,
            [(a, core, b, core) for a, b in routes[d] for core in (0, 1)],
        )
        for d in distances
    ]
    swapped = [swap(block) for block in first]
    q = pl.pallas_call(
        load_kernel,
        out_shape=pltpu.VMEM((tokens, QH * HD), jnp.bfloat16),
        in_specs=[any_spec],
        out_specs=vmem_spec,
        scratch_shapes=[pltpu.SemaphoreType.DMA(())],
        compiler_params=params,
    )(in_hbm(queries[0]))
    first[0], q = lax.optimization_barrier((first[0], q))
    is_high = lax.axis_index("seq") // 2 // half % 2 == 1
    mixed = jnp.where(is_high, first[0], own)

    def across(step):
        return [(lo + (j - step) % half, lo + half + j) for lo in (0, group) for j in range(half)]

    back = [(half + j, j) for j in range(half) if j != 1]
    back += [(group + half + j, group + j) for j in range(2, half)]
    back += [(group + half, group + 1), (group + half + 1, 1)]
    merged = across(1) + [(half + 1, group)] + back
    both = [send(mixed, [(a, c, b, c) for a, b in merged for c in (0, 1)])]
    own_later, _ = lax.optimization_barrier((own, first[0]))
    cross = both + [
        send(own_later, [(a, c, b, c) for a, b in across(step) for c in (0, 1)])
        for step in range(2, half)
    ]
    far = []
    for j in range(half):
        if j == 1:
            far += both
            continue
        path = [half + j, group, *([group + 1] if j % 2 else []), half + j]
        far.append(
            send(first[0], [(a, c, b, c) for a, b in zip(path, path[1:]) for c in (0, 1)])
        )

    def position(source, core, tokens, valid):
        return jnp.where(valid, (2 * source + core) * tokens, never)

    def early_bases(index, tokens):
        pair, core = index // 2, index % 2
        bases = [position(pair, core, tokens, True), position(pair, 1 - core, tokens, True)]
        for d in distances:
            reached = pair // half % 2 == 1 if d == half else pair % half >= d
            for other in (core, 1 - core):
                bases.append(position(pair - d, other, tokens, reached | (pair == group)))
        return bases

    def high_bases(index, tokens):
        pair, core = index // 2, index % 2
        local = pair % half
        bases = []
        for step in range(1, half):
            source = pair - half - local + (local + half - step) % half
            bases += [position(source, other, tokens, True) for other in (core, 1 - core)]
        return bases

    def middle_bases(index, tokens):
        core = index % 2
        return [
            position(low, other, tokens, True) for low in range(half) for other in (core, 1 - core)
        ]

    lengths_row = lax.dynamic_index_in_dim(doc_lengths, lax.axis_index("dp"), 0, keepdims=False)
    positions = lax.axis_index("seq") * tokens + jnp.arange(tokens, dtype=jnp.int32)
    starts = jnp.broadcast_to(doc_starts(lengths_row, positions)[:, None], (tokens, HD))
    early = [own, sibling]
    for block, other in zip(first, swapped):
        early += [block, other]
    early = [resident(a) for a in early]
    out_scratch = [pltpu.VMEM((tokens, QH * HD), jnp.bfloat16), pltpu.SemaphoreType.DMA((KVH,))]
    result = jax.ShapeDtypeStruct((tokens, QH * HD), jnp.bfloat16)
    summed, out = pl.pallas_call(
        functools.partial(early_kernel, group, half, early_bases),
        out_shape=[pltpu.VMEM((KVH, GROUP * tokens, 2 * HD), jnp.float32), result],
        in_specs=[vmem_spec] * (2 + len(early)),
        out_specs=[vmem_spec, any_spec],
        scratch_shapes=out_scratch,
        compiler_params=params,
        cost_estimate=pl.CostEstimate(flops=1, bytes_accessed=1, transcendentals=0),
    )(resident(q), resident(starts), *early)

    seen, arrived = {}, []
    for blocks in (far, cross):
        held = []
        for block in blocks:
            if id(block) not in seen:
                tied, summed = lax.optimization_barrier((block, summed))
                seen[id(block)] = [resident(tied), resident(swap(tied))]
            held += seen[id(block)]
        arrived.append(held)
    middle, high = arrived
    for reads, rows, bases, late in (
        (lambda pair: pair // half % 2 == 1, tokens, high_bases, high),
        (lambda pair: pair == group, tokens // 2, middle_bases, middle),
    ):
        out = pl.pallas_call(
            functools.partial(late_kernel, reads, rows, early_bases, bases),
            out_shape=result,
            in_specs=[vmem_spec] * 3 + [[vmem_spec] * len(a) for a in (early, late)] + [any_spec],
            out_specs=any_spec,
            scratch_shapes=out_scratch,
            input_output_aliases={3 + len(early) + len(late): 0},
            compiler_params=params,
            cost_estimate=pl.CostEstimate(flops=1, bytes_accessed=1, transcendentals=0),
        )(resident(q), resident(starts), resident(summed), early, late, out)
    return out[None]


def solution(mesh):
    placed = (P("dp", "seq", None), P("dp", "seq", None), P("dp", "seq", None), P())
    return jax.shard_map(
        per_device, mesh=mesh, in_specs=placed, out_specs=P("dp", "seq", None), check_vma=False
    )
```

```python
import functools
import math

import jax
import jax.numpy as jnp
from jax import lax
from jax.experimental import pallas as pl
from jax.experimental.pallas import tpu as pltpu
from jax.sharding import PartitionSpec as P

QH = 64
KVH = 8
HD = 128
GROUP = 8
WIDE = GROUP * HD
MASKED = -1e30
EXPONENT_SCALE = math.log2(math.e) / math.sqrt(HD)
LOW_TOTAL, HIGH_TOTAL = 2.0**-60, 2.0**80
MARK_BYTES = 64 * 1024 * 1024
VMEM_LIMIT = 24 * 1024 * 1024


def join_kernel(keys, values, joined, sems):
    copies = [
        pltpu.make_async_copy(keys, joined.at[:, : KVH * HD], sems.at[0]),
        pltpu.make_async_copy(values, joined.at[:, KVH * HD :], sems.at[1]),
    ]
    for copy in copies:
        copy.start()
    for copy in copies:
        copy.wait()


def doc_starts(lengths_row, positions):
    doc_ends = jnp.cumsum(lengths_row)
    return jnp.max(jnp.where(doc_ends[None, :] <= positions[:, None], doc_ends, 0), axis=1)


def columns(first, width=HD):
    return pl.ds(first if isinstance(first, int) else pl.multiple_of(first, HD), width)


def mask_of(first, rows, tokens, bases, first_position, starts):
    row_position = first_position + first + lax.broadcasted_iota(jnp.int32, (rows, tokens), 0)
    column = lax.broadcasted_iota(jnp.int32, (rows, tokens), 1)
    begin = starts[first : first + rows, :tokens]
    parts = []
    for base in bases:
        key_position = base + column
        allowed = (key_position >= begin) & (key_position <= row_position)
        parts.append(jnp.where(allowed, 0.0, MASKED))
    return jnp.concatenate(parts, axis=1)


def exponents_of(g, first, rows, q, blocks, mask):
    q_rows = jnp.concatenate(
        [q[first : first + rows, columns((g * GROUP + h) * HD)] for h in range(GROUP)], axis=0
    )
    k = jnp.concatenate([b[:, columns(g * HD)] for b in blocks], axis=0)
    scores = lax.dot_general(
        q_rows, k, (((1,), (1,)), ((), ())), preferred_element_type=jnp.float32
    )
    masked = scores.reshape(GROUP, rows, -1) + mask[None]
    return masked.reshape(scores.shape) * EXPONENT_SCALE


def weighted_sum(g, exponents, blocks):
    v = jnp.concatenate([b[:, columns((KVH + g) * HD)] for b in blocks], axis=0)
    v = jnp.concatenate([v, jnp.ones_like(v)], axis=1)
    weights = jnp.exp2(exponents).astype(jnp.bfloat16)
    return jnp.dot(weights, v, preferred_element_type=jnp.float32)


def mark_kernel(block, mark):
    mark[...] = block[:16, :HD]


def load_kernel(source, target, sem):
    copy = pltpu.make_async_copy(source, target, sem)
    copy.start()
    copy.wait()


def copy_out(g, out, out_hbm, sems):
    part = columns(g * WIDE, WIDE)
    return pltpu.make_async_copy(out.at[:, part], out_hbm.at[:, part], sems.at[g])


def store(g, first, total, out):
    rows = total.shape[0] // GROUP
    result = (total[:, :HD] / total[:, HD:]).astype(jnp.bfloat16)
    for h in range(GROUP):
        out[first : first + rows, columns((g * GROUP + h) * HD)] = result[h * rows : (h + 1) * rows]


def finish(totals_of, spans, q, starts, first_position, out, out_hbm, sems):
    tokens = q.shape[0]
    lowest = highest = jnp.ones((GROUP * tokens, HD), jnp.float32)
    for g in range(KVH):
        totals = totals_of(g)
        for (first, *_), total in zip(spans, totals):
            store(g, first, total, out)
        weights = jnp.concatenate([total[:, HD:] for total in totals], axis=0)
        lowest, highest = jnp.minimum(lowest, weights), jnp.maximum(highest, weights)
        copy_out(g, out, out_hbm, sems).start()
    any_fault = jnp.max(jnp.maximum(LOW_TOTAL / lowest, highest / HIGH_TOTAL)) >= 1.0
    for g in range(KVH):
        copy_out(g, out, out_hbm, sems).wait()

    @pl.when(any_fault)
    def _():
        for first, rows, blocks, bases in spans:
            mask = mask_of(first, rows, tokens, bases, first_position, starts)

            def one(g, _):
                exponents = exponents_of(g, first, rows, q, blocks, mask)
                peak = jnp.max(exponents, axis=1, keepdims=True)
                store(g, first, weighted_sum(g, exponents - peak, blocks), out)
                return 0

            lax.fori_loop(0, KVH, one, 0)
        for g in range(KVH):
            copy_out(g, out, out_hbm, sems).start()
        for g in range(KVH):
            copy_out(g, out, out_hbm, sems).wait()


def early_kernel(group, half, base_of, q, starts, *refs):
    blocks, (summed, out_hbm, out, sems) = refs[:-4], refs[-4:]
    tokens = q.shape[0]
    index = lax.axis_index("seq")
    bases = base_of(index, tokens)
    mask = mask_of(0, tokens, tokens, bases, index * tokens, starts)
    for g in range(KVH):
        summed[g] = weighted_sum(g, exponents_of(g, 0, tokens, q, blocks, mask), blocks)
    pair = index // 2

    @pl.when((pair != group) & (pair // half % 2 == 0))
    def _():
        spans = [(0, tokens, blocks, bases)]
        finish(lambda g: [summed[g]], spans, q, starts, index * tokens, out, out_hbm, sems)


def late_kernel(
    reads, rows, base_of, late_base_of, q, starts, summed, early, late, _, out_hbm, out, sems
):
    tokens = q.shape[0]
    index = lax.axis_index("seq")

    def earlier(g, first, length):
        return jnp.concatenate(
            [summed[g, h * tokens + first : h * tokens + first + length] for h in range(GROUP)],
            axis=0,
        )

    @pl.when(reads(index // 2))
    def _():
        early_bases, bases = base_of(index, tokens), late_base_of(index, tokens)
        mask = mask_of(0, rows, tokens, bases, index * tokens, starts)
        exponents = [exponents_of(g, 0, rows, q, late, mask) for g in range(KVH)]
        new = [weighted_sum(g, exponents[g], late) for g in range(KVH)]
        spans = [(0, rows, early + late, early_bases + bases)]
        if rows < tokens:
            spans.append((rows, tokens - rows, early, early_bases))

        def totals_of(g):
            rest = [earlier(g, first, length) for first, length, *_ in spans[1:]]
            return [earlier(g, 0, rows) + new[g], *rest]

        finish(totals_of, spans, q, starts, index * tokens, out, out_hbm, sems)


def closed(routes, count):
    onward = dict(routes)
    backward = {b: a for a, b in routes}
    for device in range(count):
        sibling = device ^ 1
        if device not in onward and device not in backward and sibling not in backward:
            onward[device], backward[sibling] = sibling, device
    for device in range(count):
        if device not in onward:
            start = device
            while start in backward:
                start = backward[start]
            onward[device], backward[start] = start, device
    return sorted(onward.items())


def per_device(queries, keys, values, doc_lengths):
    tokens = queries.shape[1]
    seq_count = lax.axis_size("seq")
    pairs = seq_count // 2
    group = pairs // 2
    half = group // 2
    never = 1 << 30

    def send(block, routes):
        devices = [(2 * a + i, 2 * b + j) for a, i, b, j in routes]
        return lax.ppermute(block, "seq", closed(devices, seq_count))

    def swap(block):
        return lax.ppermute(block, "seq", [(2 * c + i, 2 * c + 1 - i) for c in range(pairs) for i in (0, 1)])

    any_spec = pl.BlockSpec(memory_space=pl.ANY)
    vmem_spec = pl.BlockSpec(memory_space=pltpu.VMEM)
    params = pltpu.CompilerParams(vmem_limit_bytes=VMEM_LIMIT)

    def in_hbm(array):
        return pltpu.with_memory_space_constraint(array, pltpu.HBM)

    def resident(array):
        return pltpu.with_memory_space_constraint(array, pltpu.VMEM)

    own = pl.pallas_call(
        join_kernel,
        out_shape=pltpu.VMEM((tokens, 2 * KVH * HD), jnp.bfloat16),
        in_specs=[any_spec] * 2,
        out_specs=vmem_spec,
        scratch_shapes=[pltpu.SemaphoreType.DMA((2,))],
        compiler_params=params,
    )(in_hbm(keys[0]), in_hbm(values[0]))

    halves = [(first, first + half) for first in range(0, pairs, half)]
    up = [(c, c + half) for c in [*range(half + 1), *range(group, group + half)]]
    along = {
        d: [(c - d, c) for lo, hi in halves for c in range(lo + d, hi)] + [(group - d, group)]
        for d in range(1, half)
    }
    routes = {half: up, **along}
    distances = [half, *along]
    sibling = swap(own)
    own_next, _ = lax.optimization_barrier((own, sibling))
    first = [
        send(
            own if d == half else own_next,
            [(a, core, b, core) for a, b in routes[d] for core in (0, 1)],
        )
        for d in distances
    ]
    swapped = [swap(block) for block in first]
    waiting, _ = lax.optimization_barrier((queries[0], sibling))
    q = pl.pallas_call(
        load_kernel,
        out_shape=pltpu.VMEM((tokens, QH * HD), jnp.bfloat16),
        in_specs=[any_spec],
        out_specs=vmem_spec,
        scratch_shapes=[pltpu.SemaphoreType.DMA(())],
        compiler_params=params,
    )(in_hbm(waiting))
    first[0], q = lax.optimization_barrier((first[0], q))
    is_high = lax.axis_index("seq") // 2 // half % 2 == 1
    mixed = jnp.where(is_high, first[0], own)
    mark = pl.pallas_call(
        mark_kernel,
        out_shape=pltpu.VMEM((16, HD), jnp.bfloat16),
        in_specs=[vmem_spec],
        out_specs=vmem_spec,
        compiler_params=params,
        cost_estimate=pl.CostEstimate(flops=0, bytes_accessed=MARK_BYTES, transcendentals=0),
    )(resident(mixed))
    came_up, _ = lax.optimization_barrier((first[0], mark))

    def across(step):
        return [(lo + (j - step) % half, lo + half + j) for lo in (0, group) for j in range(half)]

    back = [(half + j, j) for j in range(half) if j != 1]
    back += [(group + half + j, group + j) for j in range(2, half)]
    back += [(group + half, group + 1), (group + half + 1, 1)]
    merged = across(1) + [(half + 1, group)] + back
    both = [send(mixed, [(a, c, b, c) for a, b in merged for c in (0, 1)])]
    own_later, _ = lax.optimization_barrier((own, first[0]))
    cross = both + [
        send(own_later, [(a, c, b, c) for a, b in across(step) for c in (0, 1)])
        for step in range(2, half)
    ]
    far = []
    for j in range(half):
        if j == 1:
            far += both
            continue
        path = [half + j, group, *([group + 1] if j % 2 else []), half + j]
        far.append(
            send(came_up, [(a, c, b, c) for a, b in zip(path, path[1:]) for c in (0, 1)])
        )

    def position(source, core, tokens, valid):
        return jnp.where(valid, (2 * source + core) * tokens, never)

    def early_bases(index, tokens):
        pair, core = index // 2, index % 2
        bases = [position(pair, core, tokens, True), position(pair, 1 - core, tokens, True)]
        for d in distances:
            reached = pair // half % 2 == 1 if d == half else pair % half >= d
            for other in (core, 1 - core):
                bases.append(position(pair - d, other, tokens, reached | (pair == group)))
        return bases

    def high_bases(index, tokens):
        pair, core = index // 2, index % 2
        local = pair % half
        bases = []
        for step in range(1, half):
            source = pair - half - local + (local + half - step) % half
            bases += [position(source, other, tokens, True) for other in (core, 1 - core)]
        return bases

    def middle_bases(index, tokens):
        core = index % 2
        return [
            position(low, other, tokens, True) for low in range(half) for other in (core, 1 - core)
        ]

    lengths_row = lax.dynamic_index_in_dim(doc_lengths, lax.axis_index("dp"), 0, keepdims=False)
    positions = lax.axis_index("seq") * tokens + jnp.arange(tokens, dtype=jnp.int32)
    starts = jnp.broadcast_to(doc_starts(lengths_row, positions)[:, None], (tokens, HD))
    early = [own, sibling]
    for block, other in zip(first, swapped):
        early += [block, other]
    early = [resident(a) for a in early]
    out_scratch = [pltpu.VMEM((tokens, QH * HD), jnp.bfloat16), pltpu.SemaphoreType.DMA((KVH,))]
    result = jax.ShapeDtypeStruct((tokens, QH * HD), jnp.bfloat16)
    summed, out = pl.pallas_call(
        functools.partial(early_kernel, group, half, early_bases),
        out_shape=[pltpu.VMEM((KVH, GROUP * tokens, 2 * HD), jnp.float32), result],
        in_specs=[vmem_spec] * (2 + len(early)),
        out_specs=[vmem_spec, any_spec],
        scratch_shapes=out_scratch,
        compiler_params=params,
        cost_estimate=pl.CostEstimate(flops=1, bytes_accessed=1, transcendentals=0),
    )(resident(q), resident(starts), *early)

    seen, arrived = {}, []
    for blocks in (cross, far):
        held = []
        for block in blocks:
            if id(block) not in seen:
                tied, summed = lax.optimization_barrier((block, summed))
                seen[id(block)] = [resident(tied), resident(swap(tied))]
            held += seen[id(block)]
        arrived.append(held)
    high, middle = arrived
    for reads, rows, bases, late in (
        (lambda pair: pair // half % 2 == 1, tokens, high_bases, high),
        (lambda pair: pair == group, tokens // 2, middle_bases, middle),
    ):
        out = pl.pallas_call(
            functools.partial(late_kernel, reads, rows, early_bases, bases),
            out_shape=result,
            in_specs=[vmem_spec] * 3 + [[vmem_spec] * len(a) for a in (early, late)] + [any_spec],
            out_specs=any_spec,
            scratch_shapes=out_scratch,
            input_output_aliases={3 + len(early) + len(late): 0},
            compiler_params=params,
            cost_estimate=pl.CostEstimate(flops=1, bytes_accessed=1, transcendentals=0),
        )(resident(q), resident(starts), resident(summed), early, late, out)
    return out[None]


def solution(mesh):
    placed = (P("dp", "seq", None), P("dp", "seq", None), P("dp", "seq", None), P())
    return jax.shard_map(
        per_device, mesh=mesh, in_specs=placed, out_specs=P("dp", "seq", None), check_vma=False
    )
```

```python
import functools
import math

import jax
import jax.numpy as jnp
from jax import lax
from jax.experimental import pallas as pl
from jax.experimental.pallas import tpu as pltpu
from jax.sharding import PartitionSpec as P

QH = 64
KVH = 8
HD = 128
GROUP = 8
WIDE = GROUP * HD
MASKED = -1e30
EXPONENT_SCALE = math.log2(math.e) / math.sqrt(HD)
LOW_TOTAL, HIGH_TOTAL = 2.0**-60, 2.0**80
MARK_BYTES = 64 * 1024 * 1024
VMEM_LIMIT = 24 * 1024 * 1024


def join_kernel(keys, values, joined, sems):
    parts = sems.shape[0]
    rows = keys.shape[0] // parts
    copies = []
    for part in range(parts):
        span = slice(part * rows, (part + 1) * rows)
        for side, source in enumerate((keys, values)):
            target = joined.at[span, side * KVH * HD : (side + 1) * KVH * HD]
            copies.append(pltpu.make_async_copy(source.at[span], target, sems.at[part, side]))
    for copy in copies:
        copy.start()
    for copy in copies:
        copy.wait()


def doc_starts(lengths_row, positions):
    doc_ends = jnp.cumsum(lengths_row)
    return jnp.max(jnp.where(doc_ends[None, :] <= positions[:, None], doc_ends, 0), axis=1)


def columns(first, width=HD):
    return pl.ds(first if isinstance(first, int) else pl.multiple_of(first, HD), width)


def mask_of(first, rows, tokens, bases, first_position, starts):
    row_position = first_position + first + lax.broadcasted_iota(jnp.int32, (rows, tokens), 0)
    column = lax.broadcasted_iota(jnp.int32, (rows, tokens), 1)
    begin = starts[first : first + rows, :tokens]
    parts = []
    for base in bases:
        key_position = base + column
        allowed = (key_position >= begin) & (key_position <= row_position)
        parts.append(jnp.where(allowed, 0.0, MASKED))
    return jnp.concatenate(parts, axis=1)


def exponents_of(g, first, rows, q, blocks, mask):
    q_rows = jnp.concatenate(
        [q[first : first + rows, columns((g * GROUP + h) * HD)] for h in range(GROUP)], axis=0
    )
    k = jnp.concatenate([b[:, columns(g * HD)] for b in blocks], axis=0)
    scores = lax.dot_general(
        q_rows, k, (((1,), (1,)), ((), ())), preferred_element_type=jnp.float32
    )
    masked = scores.reshape(GROUP, rows, -1) + mask[None]
    return masked.reshape(scores.shape) * EXPONENT_SCALE


def weighted_sum(g, exponents, blocks):
    v = jnp.concatenate([b[:, columns((KVH + g) * HD)] for b in blocks], axis=0)
    v = jnp.concatenate([v, jnp.ones_like(v)], axis=1)
    weights = jnp.exp2(exponents).astype(jnp.bfloat16)
    return jnp.dot(weights, v, preferred_element_type=jnp.float32)


def mark_kernel(block, mark):
    mark[...] = block[:16, :HD]


def load_kernel(source, target, sem):
    copy = pltpu.make_async_copy(source, target, sem)
    copy.start()
    copy.wait()


def copy_out(g, out, out_hbm, sems):
    part = columns(g * WIDE, WIDE)
    return pltpu.make_async_copy(out.at[:, part], out_hbm.at[:, part], sems.at[g])


def store(g, first, total, out):
    rows = total.shape[0] // GROUP
    result = (total[:, :HD] / total[:, HD:]).astype(jnp.bfloat16)
    for h in range(GROUP):
        out[first : first + rows, columns((g * GROUP + h) * HD)] = result[h * rows : (h + 1) * rows]


def finish(totals_of, spans, q, starts, first_position, out, out_hbm, sems):
    tokens = q.shape[0]
    lowest = highest = jnp.ones((GROUP * tokens, HD), jnp.float32)
    for g in range(KVH):
        totals = totals_of(g)
        for (first, *_), total in zip(spans, totals):
            store(g, first, total, out)
        weights = jnp.concatenate([total[:, HD:] for total in totals], axis=0)
        lowest, highest = jnp.minimum(lowest, weights), jnp.maximum(highest, weights)
        copy_out(g, out, out_hbm, sems).start()
    any_fault = jnp.max(jnp.maximum(LOW_TOTAL / lowest, highest / HIGH_TOTAL)) >= 1.0
    for g in range(KVH):
        copy_out(g, out, out_hbm, sems).wait()

    @pl.when(any_fault)
    def _():
        for first, rows, blocks, bases in spans:
            mask = mask_of(first, rows, tokens, bases, first_position, starts)

            def one(g, _):
                exponents = exponents_of(g, first, rows, q, blocks, mask)
                peak = jnp.max(exponents, axis=1, keepdims=True)
                store(g, first, weighted_sum(g, exponents - peak, blocks), out)
                return 0

            lax.fori_loop(0, KVH, one, 0)
        for g in range(KVH):
            copy_out(g, out, out_hbm, sems).start()
        for g in range(KVH):
            copy_out(g, out, out_hbm, sems).wait()


def early_kernel(group, half, base_of, q, starts, *refs):
    blocks, (summed, out_hbm, out, sems) = refs[:-4], refs[-4:]
    tokens = q.shape[0]
    index = lax.axis_index("seq")
    bases = base_of(index, tokens)
    mask = mask_of(0, tokens, tokens, bases, index * tokens, starts)
    for g in range(KVH):
        summed[g] = weighted_sum(g, exponents_of(g, 0, tokens, q, blocks, mask), blocks)
    pair = index // 2

    @pl.when((pair != group) & (pair // half % 2 == 0))
    def _():
        spans = [(0, tokens, blocks, bases)]
        finish(lambda g: [summed[g]], spans, q, starts, index * tokens, out, out_hbm, sems)


def late_kernel(
    reads, rows, base_of, late_base_of, q, starts, summed, early, late, _, out_hbm, out, sems
):
    tokens = q.shape[0]
    index = lax.axis_index("seq")

    def earlier(g, first, length):
        return jnp.concatenate(
            [summed[g, h * tokens + first : h * tokens + first + length] for h in range(GROUP)],
            axis=0,
        )

    @pl.when(reads(index // 2))
    def _():
        early_bases, bases = base_of(index, tokens), late_base_of(index, tokens)
        mask = mask_of(0, rows, tokens, bases, index * tokens, starts)
        exponents = [exponents_of(g, 0, rows, q, late, mask) for g in range(KVH)]
        new = [weighted_sum(g, exponents[g], late) for g in range(KVH)]
        spans = [(0, rows, early + late, early_bases + bases)]
        if rows < tokens:
            spans.append((rows, tokens - rows, early, early_bases))

        def totals_of(g):
            rest = [earlier(g, first, length) for first, length, *_ in spans[1:]]
            return [earlier(g, 0, rows) + new[g], *rest]

        finish(totals_of, spans, q, starts, index * tokens, out, out_hbm, sems)


def closed(routes, count):
    onward = dict(routes)
    backward = {b: a for a, b in routes}
    for device in range(count):
        sibling = device ^ 1
        if device not in onward and device not in backward and sibling not in backward:
            onward[device], backward[sibling] = sibling, device
    for device in range(count):
        if device not in onward:
            start = device
            while start in backward:
                start = backward[start]
            onward[device], backward[start] = start, device
    return sorted(onward.items())


def per_device(queries, keys, values, doc_lengths):
    tokens = queries.shape[1]
    seq_count = lax.axis_size("seq")
    pairs = seq_count // 2
    group = pairs // 2
    half = group // 2
    never = 1 << 30

    def send(block, routes):
        devices = [(2 * a + i, 2 * b + j) for a, i, b, j in routes]
        return lax.ppermute(block, "seq", closed(devices, seq_count))

    def swap(block):
        return lax.ppermute(block, "seq", [(2 * c + i, 2 * c + 1 - i) for c in range(pairs) for i in (0, 1)])

    any_spec = pl.BlockSpec(memory_space=pl.ANY)
    vmem_spec = pl.BlockSpec(memory_space=pltpu.VMEM)
    params = pltpu.CompilerParams(vmem_limit_bytes=VMEM_LIMIT)

    def in_hbm(array):
        return pltpu.with_memory_space_constraint(array, pltpu.HBM)

    def resident(array):
        return pltpu.with_memory_space_constraint(array, pltpu.VMEM)

    own = pl.pallas_call(
        join_kernel,
        out_shape=pltpu.VMEM((tokens, 2 * KVH * HD), jnp.bfloat16),
        in_specs=[any_spec] * 2,
        out_specs=vmem_spec,
        scratch_shapes=[pltpu.SemaphoreType.DMA((tokens // 16, 2))],
        compiler_params=params,
    )(in_hbm(keys[0]), in_hbm(values[0]))

    halves = [(first, first + half) for first in range(0, pairs, half)]
    up = [(c, c + half) for c in [*range(half + 1), *range(group, group + half)]]
    along = {
        d: [(c - d, c) for lo, hi in halves for c in range(lo + d, hi)] + [(group - d, group)]
        for d in range(1, half)
    }
    routes = {half: up, **along}
    distances = [half, *along]
    sibling = swap(own)
    own_next, _ = lax.optimization_barrier((own, sibling))
    first = [
        send(
            own if d == half else own_next,
            [(a, core, b, core) for a, b in routes[d] for core in (0, 1)],
        )
        for d in distances
    ]
    swapped = [swap(block) for block in first]
    waiting, _ = lax.optimization_barrier((queries[0], sibling))
    q = pl.pallas_call(
        load_kernel,
        out_shape=pltpu.VMEM((tokens, QH * HD), jnp.bfloat16),
        in_specs=[any_spec],
        out_specs=vmem_spec,
        scratch_shapes=[pltpu.SemaphoreType.DMA(())],
        compiler_params=params,
    )(in_hbm(waiting))
    first[0], q = lax.optimization_barrier((first[0], q))
    is_high = lax.axis_index("seq") // 2 // half % 2 == 1
    mixed = jnp.where(is_high, first[0], own)
    mark = pl.pallas_call(
        mark_kernel,
        out_shape=pltpu.VMEM((16, HD), jnp.bfloat16),
        in_specs=[vmem_spec],
        out_specs=vmem_spec,
        compiler_params=params,
        cost_estimate=pl.CostEstimate(flops=0, bytes_accessed=MARK_BYTES, transcendentals=0),
    )(resident(mixed))
    came_up, _ = lax.optimization_barrier((first[0], mark))

    def across(step):
        return [(lo + (j - step) % half, lo + half + j) for lo in (0, group) for j in range(half)]

    back = [(half + j, j) for j in range(half) if j != 1]
    back += [(group + half + j, group + j) for j in range(2, half)]
    back += [(group + half, group + 1), (group + half + 1, 1)]
    merged = across(1) + [(half + 1, group)] + back
    both = [send(mixed, [(a, c, b, c) for a, b in merged for c in (0, 1)])]
    own_later, _ = lax.optimization_barrier((own, first[0]))
    cross = both + [
        send(own_later, [(a, c, b, c) for a, b in across(step) for c in (0, 1)])
        for step in range(2, half)
    ]
    far = []
    for j in range(half):
        if j == 1:
            far += both
            continue
        path = [half + j, group, *([group + 1] if j % 2 else []), half + j]
        far.append(
            send(came_up, [(a, c, b, c) for a, b in zip(path, path[1:]) for c in (0, 1)])
        )

    def position(source, core, tokens, valid):
        return jnp.where(valid, (2 * source + core) * tokens, never)

    def early_bases(index, tokens):
        pair, core = index // 2, index % 2
        bases = [position(pair, core, tokens, True), position(pair, 1 - core, tokens, True)]
        for d in distances:
            reached = pair // half % 2 == 1 if d == half else pair % half >= d
            for other in (core, 1 - core):
                bases.append(position(pair - d, other, tokens, reached | (pair == group)))
        return bases

    def high_bases(index, tokens):
        pair, core = index // 2, index % 2
        local = pair % half
        bases = []
        for step in range(1, half):
            source = pair - half - local + (local + half - step) % half
            bases += [position(source, other, tokens, True) for other in (core, 1 - core)]
        return bases

    def middle_bases(index, tokens):
        core = index % 2
        return [
            position(low, other, tokens, True) for low in range(half) for other in (core, 1 - core)
        ]

    lengths_row = lax.dynamic_index_in_dim(doc_lengths, lax.axis_index("dp"), 0, keepdims=False)
    positions = lax.axis_index("seq") * tokens + jnp.arange(tokens, dtype=jnp.int32)
    starts = jnp.broadcast_to(doc_starts(lengths_row, positions)[:, None], (tokens, HD))
    early = [own, sibling]
    for block, other in zip(first, swapped):
        early += [block, other]
    early = [resident(a) for a in early]
    out_scratch = [pltpu.VMEM((tokens, QH * HD), jnp.bfloat16), pltpu.SemaphoreType.DMA((KVH,))]
    result = jax.ShapeDtypeStruct((tokens, QH * HD), jnp.bfloat16)
    summed, out = pl.pallas_call(
        functools.partial(early_kernel, group, half, early_bases),
        out_shape=[pltpu.VMEM((KVH, GROUP * tokens, 2 * HD), jnp.float32), result],
        in_specs=[vmem_spec] * (2 + len(early)),
        out_specs=[vmem_spec, any_spec],
        scratch_shapes=out_scratch,
        compiler_params=params,
        cost_estimate=pl.CostEstimate(flops=1, bytes_accessed=1, transcendentals=0),
    )(resident(q), resident(starts), *early)

    seen, arrived = {}, []
    for blocks in (cross, far):
        held = []
        for block in blocks:
            if id(block) not in seen:
                tied, summed = lax.optimization_barrier((block, summed))
                seen[id(block)] = [resident(tied), resident(swap(tied))]
            held += seen[id(block)]
        arrived.append(held)
    high, middle = arrived
    for reads, rows, bases, late in (
        (lambda pair: pair // half % 2 == 1, tokens, high_bases, high),
        (lambda pair: pair == group, tokens // 2, middle_bases, middle),
    ):
        out = pl.pallas_call(
            functools.partial(late_kernel, reads, rows, early_bases, bases),
            out_shape=result,
            in_specs=[vmem_spec] * 3 + [[vmem_spec] * len(a) for a in (early, late)] + [any_spec],
            out_specs=any_spec,
            scratch_shapes=out_scratch,
            input_output_aliases={3 + len(early) + len(late): 0},
            compiler_params=params,
            cost_estimate=pl.CostEstimate(flops=1, bytes_accessed=1, transcendentals=0),
        )(resident(q), resident(starts), resident(summed), early, late, out)
    return out[None]


def solution(mesh):
    placed = (P("dp", "seq", None), P("dp", "seq", None), P("dp", "seq", None), P())
    return jax.shard_map(
        per_device, mesh=mesh, in_specs=placed, out_specs=P("dp", "seq", None), check_vma=False
    )
```
